128 devices in a mesh: rep: 8 (over y, x_lo), row: 16 (over x_hi, z, core).
Axes of the slice: x: 4 (x_hi: 2, x_lo: 2; x = x_hi * 2 + x_lo), y: 4, z: 4, core: 2. Of those that a mesh axis runs over, the one named last changes fastest.
Arguments:
- features: bfloat16 [262144, 128], P(('rep', 'row')), may hold values from -6 to 6
- degrees: int32 [262144], P(('rep', 'row')), may hold values from 4 to 128
- tile_values: bfloat16 [98304, 128, 128], P(('rep', 'row')), may hold values from 0 to 3, as said below
- tile_rows: int32 [98304], P(('rep', 'row')), may hold values from 0 to 127
- tile_cols: int32 [98304], P(('rep', 'row')), may hold values from 0 to 255
- tile_live: int32 [128], P(('rep', 'row')), may hold values from 384 to 768, as said below
- weight: bfloat16 [128, 128], replicated, may hold values from -0.5 to 0.5
- bias: float32 [128], replicated, may hold values from -1 to 1
Outputs:
- activations: bfloat16 [262144, 128], P(('rep', 'row'))
The draws below stay inside these ranges and needn't reach their ends.
Inputs may be any that keep to these rules, and one draw needn't show every extreme that they name: `tile_live`: at least one device has all 768 slots live. `tile_values`: sparse tiles of small integer edge counts, mostly zeros and ones.
All inputs are finite; a program needn't handle non-finite values.
Results may differ from the reference program's by a relative error of at most 0.0053.
Values may be sent and summed in bfloat16 or wider, within the bound.
A program may use at most 256 MiB of HBM per device.

```python
import jax
import jax.numpy as jnp
from jax import lax

F = 128
NBD = 2048
TILES_DEV = 768
NODES = 262144
ALL_TILES = 98304
N_REP = 8
N_ROW = 16


def draw_tile_values(key, part):
    key = jax.random.fold_in(key, 3)
    level = jax.random.uniform(key, (N_REP * N_ROW * TILES_DEV, 128, 128), jnp.float32)
    counts = jnp.where(level < 0.016, 1.0, jnp.where(level < 0.019, 2.0, jnp.where(level < 0.02, 3.0, 0.0)))
    return counts.astype(jnp.float32).astype(jnp.bfloat16)


def draw_tile_live(key, part):
    key = jax.random.fold_in(key, 7)
    first, second = jax.random.split(key)
    counts = jax.random.randint(first, (N_REP * N_ROW,), max(1, TILES_DEV // 2), TILES_DEV + 1)
    chosen = jax.random.randint(second, (), 0, N_REP * N_ROW)
    return counts.at[chosen].set(TILES_DEV)


def place_ends(array, key, smallest, high):
    index_at = [jax.random.randint(jax.random.fold_in(key, axis), (), 0, length) for axis, length in enumerate(array.shape)]
    widest = array.shape.index(max(array.shape))
    beside = index_at[:widest] + [(index_at[widest] + 1) % array.shape[widest]] + index_at[widest + 1:]
    return array.at[tuple(index_at)].set(smallest).at[tuple(beside)].set(high)


def shard_levels(stream_key, shape, shards, low, largest):
    level, own = 1.0, jax.random.fold_in(stream_key, 6)
    for axis_at, shards_of in shards:
        draws = jnp.exp(jax.random.uniform(jax.random.fold_in(own, axis_at), (shards_of,), jnp.float32, low / len(shards), largest / len(shards)))
        level = level * jnp.repeat(draws, shape[axis_at] // shards_of).reshape([-1 if axis == axis_at else 1 for axis in range(len(shape))])
    return level


def normal_values(own_key, shape, deviation, bound, shards=(), kind=jnp.bfloat16):
    drawn = deviation * jax.random.normal(own_key, shape, jnp.float32)
    if shards:
        drawn = drawn * shard_levels(own_key, shape, shards, -0.22, 0.18)
    return jnp.clip(drawn, -bound, bound).astype(kind)


def setup_inputs(seed: int = 0) -> dict:
    keys = jax.random.split(jax.random.key(seed), 9)
    features = normal_values(keys[0], (NODES, F), 1.0, 6.0, ((0, 128),))
    degrees = place_ends(jax.random.randint(keys[1], (NODES,), 4, 129), jax.random.fold_in(keys[1], 1), 4, 128).astype(jnp.int32)
    tile_values = draw_tile_values(jax.random.fold_in(keys[8], 71), 0)
    tile_rows = place_ends(jax.random.randint(keys[3], (ALL_TILES,), 0, N_REP * (NBD // 128)), jax.random.fold_in(keys[3], 1), 0, (N_REP * (NBD // 128)) - 1).astype(jnp.int32)
    tile_cols = place_ends(jax.random.randint(keys[4], (ALL_TILES,), 0, N_ROW * (NBD // 128)), jax.random.fold_in(keys[4], 1), 0, (N_ROW * (NBD // 128)) - 1).astype(jnp.int32)
    tile_live = draw_tile_live(jax.random.fold_in(keys[8], 71), 0)
    weight = normal_values(keys[6], (F, F), F ** -0.5, 0.5)
    bias = normal_values(keys[7], (F,), 0.25, 1.0, (), jnp.float32)
    return dict(features=features, degrees=degrees, tile_values=tile_values, tile_rows=tile_rows, tile_cols=tile_cols, tile_live=tile_live, weight=weight, bias=bias)


def reference(features, degrees, tile_values, tile_rows, tile_cols, tile_live, weight, bias):
    nbt = NBD // 128
    count = N_REP * N_ROW
    scale = lax.rsqrt(degrees.astype(jnp.float32))
    scaled = (features.astype(jnp.float32) * scale[:, None]).astype(jnp.bfloat16)
    blocks = scaled.reshape(NODES // 128, 128, F)
    values = tile_values.reshape(count, TILES_DEV, 128, 128)
    rows = tile_rows.reshape(count, TILES_DEV)
    cols = tile_cols.reshape(count, TILES_DEV)
    slots = jnp.arange(TILES_DEV, dtype=jnp.int32)

    def step(total, item):
        vals, row_ids, col_ids, live, device = item
        group = device // N_ROW
        inner = device % N_ROW
        grow = (row_ids // nbt * N_ROW + inner) * nbt + row_ids % nbt
        gcol = (group * N_ROW + col_ids // nbt) * nbt + col_ids % nbt
        picked = blocks[gcol].astype(jnp.float32)
        prods = jnp.einsum('kab,kbf->kaf', vals.astype(jnp.float32), picked)
        prods = prods * (slots < live).astype(jnp.float32)[:, None, None]
        return (total.at[grow].add(prods), None)
    start = jnp.zeros((NODES // 128, 128, F), jnp.float32)
    summed, _ = lax.scan(step, start, (values, rows, cols, tile_live, jnp.arange(count, dtype=jnp.int32)))
    aggregated = (summed.reshape(NODES, F) * scale[:, None]).astype(jnp.bfloat16)
    mixed = jnp.dot(aggregated, weight, preferred_element_type=jnp.float32) + bias[None, :]
    return jax.nn.relu(mixed).astype(jnp.bfloat16)
```

```python
import functools

import jax
import jax.numpy as jnp
from jax import lax
from jax.experimental import pallas as pl
from jax.experimental.pallas import tpu as pltpu
from jax.sharding import PartitionSpec as P

MESH = pl.DeviceIdType.MESH
F32, BF16, I32 = jnp.float32, jnp.bfloat16, jnp.int32
NT = (((1,), (1,)), ((), ()))
TN = (((0,), (0,)), ((), ()))

T = 128
CH = 2
FC = 128 // CH
SLOTS = 768
STEPS = 448
UNROLL = 32
ITERS = STEPS // UNROLL
NX = 2
NA = 6
NB = 16 - NA
HA, HB = NA // 2, NB // 2
ROW_KEEP, ROW_END = 8, 12


def make_plan(rows_ref, cols_ref, live, plan_ref):
    lane = lax.broadcasted_iota(I32, (T, T), 1)
    sub = lax.broadcasted_iota(I32, (T, T), 0)
    before = (sub < lane).astype(BF16)
    lane1 = lax.broadcasted_iota(I32, (1, T), 1)
    lane_f = lane.astype(F32)
    zero = jnp.zeros((T, T), F32)
    carry = jnp.zeros((T, 1), F32)
    hots, ranks, alive = [], [], []
    for j in range(SLOTS // T):
        there = (lane1 + j * T) < live
        r = jnp.where(there, rows_ref[j : j + 1, :], T)
        hot = jnp.where(sub == r, 1.0, 0.0).astype(F32)
        earlier = jnp.dot(hot.astype(BF16), before, preferred_element_type=F32)
        ranks.append(jnp.sum(hot * (earlier + carry), axis=0, keepdims=True))
        carry = carry + jnp.sum(hot, axis=1, keepdims=True)
        hots.append(hot)
        alive.append(there)
    pairs = jnp.broadcast_to(jnp.floor((carry + 1.0) * 0.5), (T, T))
    start = jnp.sum(jnp.where(lane < sub, pairs.T, zero), axis=1, keepdims=True)
    start = jnp.broadcast_to(start, (T, T))
    places, codes = [], []
    for j in range(SLOTS // T):
        place = ranks[j] + 2.0 * jnp.sum(hots[j] * start, axis=0, keepdims=True)
        places.append(jnp.where(alive[j], place, -1.0))
        codes.append(((lane1 + (j * T - SLOTS)) * 256 + cols_ref[j : j + 1, :]).astype(F32))
    fill = [jnp.full((2, T), -1.0, F32)]
    places_t = jnp.concatenate(places + fill, axis=0).T
    codes_t = jnp.concatenate(codes + fill, axis=0).T
    sums = [zero] * (2 * STEPS // T)
    for j in range(SLOTS // T):
        place = jnp.broadcast_to(places_t[:, j : j + 1], (T, T))
        code = jnp.broadcast_to(codes_t[:, j : j + 1], (T, T))
        for b in range(2 * STEPS // T):
            sums[b] = sums[b] + jnp.where(place == lane_f + float(b * T), code, zero)
    for b in range(2 * STEPS // T):
        code = jnp.sum(sums[b], axis=0, keepdims=True).astype(I32) + SLOTS * 256
        plan_ref[b : b + 1, :] = jnp.clip(code, 0, SLOTS * 256 + 255)
    for b in range(4):
        begins = jnp.where((start == lane_f + float(b * T)) & (pairs > 0.0), 1.0, 0.0)
        plan_ref[ROW_KEEP + b : ROW_KEEP + b + 1, :] = 1 - jnp.sum(begins, axis=0, keepdims=True).astype(I32)
    ends = jnp.where(pairs > 0.0, start + pairs - 1.0, float(STEPS))
    plan_ref[ROW_END : ROW_END + 1, :] = jnp.clip(ends.T[0:1, :].astype(I32), 0, STEPS)


def kernel(
    feat_ref, deg_ref, tiles_ref, rows_ref, cols_ref, live_ref, weight_ref, bias_ref, out_ref,
    a_buf, x0, x1, s_buf, o0, o1, plan_v, plan_s, agg,
    rxa, rb1l, rb1h, rbm, rbp, ra1l, ra1h, ram, rap, sxb, rxb,
    a_sem, p_sem, gs, gr, rs, rr,
):
    rep, row = lax.axis_index("rep"), lax.axis_index("row")
    y, l = rep // 2, rep % 2
    h, z, c = row // 8, (row // 2) % 4, row % 2
    zp = (rep, h * 8 + ((z + 1) % 4) * 2 + c)
    zm = (rep, h * 8 + ((z + 3) % 4) * 2 + c)
    xh = (rep, (1 - h) * 8 + z * 2 + c)
    sib = (rep, h * 8 + z * 2 + (1 - c))
    xl = (y * 2 + (1 - l), row)
    yp = (((y + 1) % 4) * 2 + l, row)
    ym = (((y + 3) % 4) * 2 + l, row)
    partners = (zp, zm, xh, sib, xl, yp, ym)
    xs, outs = (x0, x1), (o0, o1)

    loads = []
    per = SLOTS // 6
    for j in range(6):
        load = pltpu.make_async_copy(
            tiles_ref.at[pl.ds(j * per, per)], a_buf.at[pl.ds(j * per, per)], a_sem.at[j]
        )
        load.start()
        loads.append(load)
    barrier = pltpu.get_barrier_semaphore()
    for device in partners:
        pl.semaphore_signal(barrier, inc=1, device_id=device, device_id_type=MESH)

    scale = lax.rsqrt(deg_ref[...].astype(F32))
    for t in range(16):
        turned = feat_ref[t * T : (t + 1) * T, :].T.astype(F32)
        scaled = (turned * scale[t : t + 1, :]).astype(BF16)
        for ch in range(CH):
            xs[ch][row * 16 + t] = scaled[ch * FC : (ch + 1) * FC, :]
    a_buf[SLOTS] = jnp.zeros((T, T), BF16)
    s_buf[STEPS] = jnp.zeros((FC, T), BF16)

    pl.semaphore_wait(barrier, len(partners))

    def block(dh, dz, core=None):
        return ((h + dh) % 2) * 8 + ((z + dz) % 4) * 2 + (c if core is None else core)

    def g_copy(ch, k, to, blk, lo=0, hi=16):
        ref = xs[ch].at[pl.ds(blk * 16 + lo, hi - lo)]
        return pltpu.make_async_remote_copy(
            ref, ref, gs.at[ch, k], gr.at[ch, k], device_id=to, device_id_type=MESH
        )

    other = 1 - c
    G = {
        0: (zp, (0, 0), (0, 3), 0, 16),
        1: (zm, (0, 0), (0, 1), 0, 16),
        2: (xh, (0, 0), (1, 0), 0, 16),
        3: (sib, (0, 0), None, 0, 16),
        4: (zp, (0, 3), (0, 2), 0, 8),
        5: (sib, (0, 3), None, 0, 16),
        6: (zm, (0, 1), (0, 2), 8, 16),
        7: (sib, (0, 1), None, 0, 16),
        8: (zp, (1, 0), (1, 3), NX, 16),
        9: (zm, (1, 0), (1, 1), NX, 16),
        10: (sib, (1, 0), None, 0, 16),
        11: (xh, (0, 2), (1, 2), 0, 8),
        12: (xh, (0, 2), (1, 2), 8, 16),
        13: (sib, (0, 2), None, 0, 8),
        14: (sib, (0, 2), None, 8, 16),
        15: (sib, (1, 3), None, NX, 16),
        16: (sib, (1, 1), None, NX, 16),
        17: (sib, (1, 2), None, 0, 8),
        18: (sib, (1, 2), None, 8, 16),
        19: (xh, (0, 3), (1, 3), 0, NX),
        20: (xh, (0, 1), (1, 1), 0, NX),
        21: (sib, (1, 3), None, 0, NX),
        22: (sib, (1, 1), None, 0, NX),
    }

    def g_send(ch, *ks):
        for k in ks:
            to, sent, _, lo, hi = G[k]
            g_copy(ch, k, to, block(*sent), lo, hi).start()

    def g_recv(ch, *ks):
        for k in ks:
            to, sent, got, lo, hi = G[k]
            blk = block(*sent, core=other) if got is None else block(*got)
            g_copy(ch, k, to, blk, lo, hi).wait_recv()

    def g_flush(ch):
        for k, (to, sent, _, lo, hi) in G.items():
            g_copy(ch, k, to, block(*sent), lo, hi).wait_send()

    def g_first(ch):
        g_send(ch, 0, 1, 2, 3)

    def g_second(ch):
        g_recv(ch, 0)
        g_send(ch, 4, 19, 5)
        g_recv(ch, 1)
        g_send(ch, 6, 20, 7)
        g_recv(ch, 2)
        g_send(ch, 8, 9, 10)

    def g_third(ch):
        g_recv(ch, 4)
        g_send(ch, 11, 13)
        g_recv(ch, 6)
        g_send(ch, 12, 14)

    def g_fourth(ch):
        g_recv(ch, 19)
        g_send(ch, 21)
        g_recv(ch, 20)
        g_send(ch, 22)
        g_recv(ch, 8)
        g_send(ch, 15)
        g_recv(ch, 9)
        g_send(ch, 16)

    def g_last(ch):
        g_recv(ch, 11)
        g_send(ch, 17)
        g_recv(ch, 12)
        g_send(ch, 18)
        g_recv(ch, 3, 5, 7, 10, 13, 14, 15, 16, 21, 22, 17, 18)

    def at_y(d):
        return (y + d) % 4

    alo, ahi = pl.ds(0, HA), pl.ds(HA, HA)
    blo, bhi = pl.ds(NA, HB), pl.ds(NA + HB, HB)
    zlo, zhi = pl.ds(0, HB), pl.ds(HB, HB)

    def r_copy(ch, k):
        o = outs[ch]
        if k < 4:
            src, dst, to = o.at[at_y(k) * 2 + (1 - l), pl.ds(0, NA)], rxa.at[ch, k], xl
        elif k < 10:
            where, part, dst, to = {
                4: (at_y(2), blo, rb1l.at[ch], ym),
                5: (at_y(2), bhi, rb1h.at[ch], yp),
                6: (at_y(1), blo, rbm.at[ch, :, zlo], yp),
                7: (at_y(3), bhi, rbp.at[ch, :, zhi], ym),
                8: (at_y(3), blo, rbp.at[ch, :, zlo], ym),
                9: (at_y(1), bhi, rbm.at[ch, :, zhi], yp),
            }[k]
            src = o.at[pl.ds(where * 2, 2), part]
        elif k < 16:
            where, part, dst, to = {
                10: (at_y(2), alo, ra1l.at[ch], ym),
                11: (at_y(2), ahi, ra1h.at[ch], yp),
                12: (at_y(1), alo, ram.at[ch, alo], yp),
                13: (at_y(3), ahi, rap.at[ch, ahi], ym),
                14: (at_y(3), alo, rap.at[ch, alo], ym),
                15: (at_y(1), ahi, ram.at[ch, ahi], yp),
            }[k]
            src = o.at[where * 2 + l, part]
        else:
            src, dst, to = sxb.at[ch], rxb.at[ch], xl
        return pltpu.make_async_remote_copy(
            src, dst, rs.at[ch, k], rr.at[ch, k], device_id=to, device_id_type=MESH
        )

    def r_send(ch, *ks):
        for k in ks:
            r_copy(ch, k).start()

    def r_recv(ch, *ks):
        for k in ks:
            r_copy(ch, k).wait_recv()

    def add_to(ch, part, at, count, got):
        o = outs[ch]

        def body(t, _):
            o[part, at + t] = (o[part, at + t].astype(F32) + got(t).astype(F32)).astype(BF16)
            return 0

        lax.fori_loop(0, count, body, 0)

    def r_first(ch):
        r_send(ch, 4, 5, 2, 6, 7, 1, 3, 0)

    def r_second(ch):
        r_recv(ch, 4)
        for side in range(2):
            add_to(ch, at_y(3) * 2 + side, NA, HB, lambda t: rb1l[ch, side, t])
        r_send(ch, 8)
        r_recv(ch, 5)
        for side in range(2):
            add_to(ch, at_y(1) * 2 + side, NA + HB, HB, lambda t: rb1h[ch, side, t])
        r_send(ch, 9)
        r_recv(ch, 2)
        add_to(ch, at_y(2) * 2 + l, 0, NA, lambda t: rxa[ch, 2, t])
        r_send(ch, 10, 11)

    def r_third(ch):
        r_recv(ch, 1)
        add_to(ch, at_y(1) * 2 + l, 0, NA, lambda t: rxa[ch, 1, t])
        r_send(ch, 12)
        r_recv(ch, 3)
        add_to(ch, at_y(3) * 2 + l, 0, NA, lambda t: rxa[ch, 3, t])
        r_send(ch, 13)

    def r_fourth(ch):
        r_recv(ch, 6, 7, 8, 9)

        def body(t, _):
            total = outs[ch][y * 2 + (1 - l), NA + t].astype(F32)
            total = total + rbm[ch, 1 - l, t].astype(F32) + rbp[ch, 1 - l, t].astype(F32)
            sxb[ch, t] = total.astype(BF16)
            return 0

        lax.fori_loop(0, NB, body, 0)
        r_send(ch, 16)

    def r_fifth(ch):
        r_recv(ch, 10)
        add_to(ch, at_y(3) * 2 + l, 0, HA, lambda t: ra1l[ch, t])
        r_send(ch, 14)
        r_recv(ch, 11)
        add_to(ch, at_y(1) * 2 + l, HA, HA, lambda t: ra1h[ch, t])
        r_send(ch, 15)

    def finish(ch, t, total):
        agg[t, ch * FC : (ch + 1) * FC, :] = (total * lax.rsqrt(deg_ref[pl.ds(t, 1), :].astype(F32))).astype(BF16)

    def r_last(ch):
        r_recv(ch, 0, 12, 13, 14, 15)

        def body_a(t, _):
            total = outs[ch][y * 2 + l, t].astype(F32) + rxa[ch, 0, t].astype(F32)
            finish(ch, t, total + ram[ch, t].astype(F32) + rap[ch, t].astype(F32))
            return 0

        lax.fori_loop(0, NA, body_a, 0)
        r_recv(ch, 16)

        def body_b(t, _):
            total = outs[ch][y * 2 + l, NA + t].astype(F32) + rxb[ch, t].astype(F32)
            finish(ch, NA + t, total + rbm[ch, l, t].astype(F32) + rbp[ch, l, t].astype(F32))
            return 0

        lax.fori_loop(0, NB, body_b, 0)

    def products(ch, events):
        x = xs[ch]

        def body(i, acc):
            for at, act in events:
                pl.when(i == at)(act)
            for u in range(UNROLL):
                spot = (i % 2) * (2 * UNROLL) + 2 * u
                first = jnp.clip(plan_s[i // 2, spot], 0, SLOTS * 256 + 255)
                second = jnp.clip(plan_s[i // 2, spot + 1], 0, SLOTS * 256 + 255)
                keep = plan_s[ROW_KEEP + i // 4, (i % 4) * UNROLL + u].astype(F32)
                values = jnp.concatenate([a_buf[first >> 8], a_buf[second >> 8]], axis=1)
                nodes = jnp.concatenate([x[first & 255], x[second & 255]], axis=1)
                acc = acc * keep + lax.dot_general(nodes, values, NT, preferred_element_type=F32)
                s_buf[i * UNROLL + u] = acc.astype(BF16)
            return acc

        lax.fori_loop(0, ITERS, body, jnp.zeros((FC, T), F32))

    def extract(ch):
        o = outs[ch]

        def body(i, _):
            for u in range(16):
                o[i, u] = s_buf[jnp.clip(plan_s[ROW_END, i * 16 + u], 0, STEPS)]
            return 0

        lax.fori_loop(0, 8, body, 0)

    g_first(0)
    make_plan(rows_ref, cols_ref, live_ref[0], plan_v)
    to_smem = pltpu.make_async_copy(plan_v, plan_s, p_sem)
    to_smem.start()
    g_second(0)
    g_third(0)
    g_first(1)
    g_fourth(0)
    to_smem.wait()
    for load in loads:
        load.wait()
    g_last(0)

    products(0, [(6, lambda: g_second(1)), (9, lambda: g_third(1)), (12, lambda: g_fourth(1))])
    extract(0)
    r_first(0)
    g_last(1)
    products(
        1,
        [
            (4, lambda: r_second(0)),
            (7, lambda: r_third(0)),
            (9, lambda: r_fourth(0)),
            (11, lambda: r_fifth(0)),
        ],
    )
    extract(1)
    r_first(1)
    r_last(0)
    r_second(1)
    r_third(1)
    r_fourth(1)
    r_fifth(1)
    r_last(1)

    def body(t, _):
        mixed = lax.dot_general(agg[t], weight_ref[...], TN, preferred_element_type=F32)
        out_ref[pl.ds(t * T, T), :] = jnp.maximum(mixed + bias_ref[...], 0.0).astype(BF16)
        return 0

    lax.fori_loop(0, 16, body, 0)
    for ch in range(CH):
        g_flush(ch)
        for k in range(17):
            r_copy(ch, k).wait_send()


def per_device(features, degrees, tile_values, tile_rows, tile_cols, tile_live, weight, bias):
    vmem = pl.BlockSpec(memory_space=pltpu.VMEM)
    tile = (FC, T)
    return pl.pallas_call(
        kernel,
        out_shape=jax.ShapeDtypeStruct(features.shape, BF16),
        in_specs=[
            vmem, vmem, pl.BlockSpec(memory_space=pl.ANY), vmem, vmem,
            pl.BlockSpec(memory_space=pltpu.SMEM), vmem, vmem,
        ],
        out_specs=vmem,
        scratch_shapes=[
            pltpu.VMEM((SLOTS + 1, T, T), BF16),
            pltpu.VMEM((256,) + tile, BF16),
            pltpu.VMEM((256,) + tile, BF16),
            pltpu.VMEM((STEPS + 1,) + tile, BF16),
            pltpu.VMEM((8, 16) + tile, BF16),
            pltpu.VMEM((8, 16) + tile, BF16),
            pltpu.VMEM((16, T), I32),
            pltpu.SMEM((16, T), I32),
            pltpu.VMEM((16, 128, T), BF16),
            pltpu.VMEM((CH, 4, NA) + tile, BF16),
            pltpu.VMEM((CH, 2, HB) + tile, BF16),
            pltpu.VMEM((CH, 2, HB) + tile, BF16),
            pltpu.VMEM((CH, 2, NB) + tile, BF16),
            pltpu.VMEM((CH, 2, NB) + tile, BF16),
            pltpu.VMEM((CH, HA) + tile, BF16),
            pltpu.VMEM((CH, HA) + tile, BF16),
            pltpu.VMEM((CH, NA) + tile, BF16),
            pltpu.VMEM((CH, NA) + tile, BF16),
            pltpu.VMEM((CH, NB) + tile, BF16),
            pltpu.VMEM((CH, NB) + tile, BF16),
            pltpu.SemaphoreType.DMA((6,)),
            pltpu.SemaphoreType.DMA,
            pltpu.SemaphoreType.DMA((CH, 23)),
            pltpu.SemaphoreType.DMA((CH, 23)),
            pltpu.SemaphoreType.DMA((CH, 17)),
            pltpu.SemaphoreType.DMA((CH, 17)),
        ],
        compiler_params=pltpu.CompilerParams(
            collective_id=0, has_side_effects=True, vmem_limit_bytes=60 << 20
        ),
        name="graph_layer",
    )(
        features,
        degrees.reshape(16, T),
        tile_values,
        tile_rows.reshape(SLOTS // T, T),
        tile_cols.reshape(SLOTS // T, T),
        tile_live,
        weight,
        bias.reshape(1, 128),
    )


def solution(mesh):
    return jax.shard_map(
        per_device,
        mesh=mesh,
        in_specs=(
            P(("rep", "row"), None),
            P(("rep", "row")),
            P(("rep", "row"), None, None),
            P(("rep", "row")),
            P(("rep", "row")),
            P(("rep", "row")),
            P(),
            P(),
        ),
        out_specs=P(("rep", "row"), None),
        check_vma=False,
    )
```

```python
import functools

import jax
import jax.numpy as jnp
from jax import lax
from jax.experimental import pallas as pl
from jax.experimental.pallas import tpu as pltpu
from jax.sharding import PartitionSpec as P

MESH = pl.DeviceIdType.MESH
F32, BF16, I32 = jnp.float32, jnp.bfloat16, jnp.int32
NT = (((1,), (1,)), ((), ()))
TN = (((0,), (0,)), ((), ()))

T = 128
CH = 2
FCS = (64, 64)
FOF = (0, FCS[0])
SLOTS = 768
STEPS = 448
UNROLL = 32
ITERS = STEPS // UNROLL
NX = 6
NQ = 4
NA = 6
NB = 16 - NA
HA, HB = NA // 2, NB // 2
ROW_KEEP, ROW_END = 8, 12


def make_plan(rows_ref, cols_ref, live, plan_ref):
    lane = lax.broadcasted_iota(I32, (T, T), 1)
    sub = lax.broadcasted_iota(I32, (T, T), 0)
    before = (sub < lane).astype(BF16)
    lane1 = lax.broadcasted_iota(I32, (1, T), 1)
    lane_f = lane.astype(F32)
    zero = jnp.zeros((T, T), F32)
    carry = jnp.zeros((T, 1), F32)
    hots, ranks, alive = [], [], []
    for j in range(SLOTS // T):
        there = (lane1 + j * T) < live
        r = jnp.where(there, rows_ref[j : j + 1, :], T)
        hot = jnp.where(sub == r, 1.0, 0.0).astype(F32)
        earlier = jnp.dot(hot.astype(BF16), before, preferred_element_type=F32)
        ranks.append(jnp.sum(hot * (earlier + carry), axis=0, keepdims=True))
        carry = carry + jnp.sum(hot, axis=1, keepdims=True)
        hots.append(hot)
        alive.append(there)
    pairs = jnp.broadcast_to(jnp.floor((carry + 1.0) * 0.5), (T, T))
    start = jnp.sum(jnp.where(lane < sub, pairs.T, zero), axis=1, keepdims=True)
    start = jnp.broadcast_to(start, (T, T))
    places, codes = [], []
    for j in range(SLOTS // T):
        place = ranks[j] + 2.0 * jnp.sum(hots[j] * start, axis=0, keepdims=True)
        places.append(jnp.where(alive[j], place, -1.0))
        codes.append(((lane1 + (j * T - SLOTS)) * 256 + cols_ref[j : j + 1, :]).astype(F32))
    fill = [jnp.full((2, T), -1.0, F32)]
    places_t = jnp.concatenate(places + fill, axis=0).T
    codes_t = jnp.concatenate(codes + fill, axis=0).T
    sums = [zero] * (2 * STEPS // T)
    for j in range(SLOTS // T):
        place = jnp.broadcast_to(places_t[:, j : j + 1], (T, T))
        code = jnp.broadcast_to(codes_t[:, j : j + 1], (T, T))
        for b in range(2 * STEPS // T):
            sums[b] = sums[b] + jnp.where(place == lane_f + float(b * T), code, zero)
    for b in range(2 * STEPS // T):
        code = jnp.sum(sums[b], axis=0, keepdims=True).astype(I32) + SLOTS * 256
        plan_ref[b : b + 1, :] = jnp.clip(code, 0, SLOTS * 256 + 255)
    for b in range(4):
        begins = jnp.where((start == lane_f + float(b * T)) & (pairs > 0.0), 1.0, 0.0)
        plan_ref[ROW_KEEP + b : ROW_KEEP + b + 1, :] = 1 - jnp.sum(begins, axis=0, keepdims=True).astype(I32)
    ends = jnp.where(pairs > 0.0, start + pairs - 1.0, float(STEPS))
    plan_ref[ROW_END : ROW_END + 1, :] = jnp.clip(ends.T[0:1, :].astype(I32), 0, STEPS)


def kernel(
    feat_ref, deg_ref, tiles_ref, rows_ref, cols_ref, live_ref, weight_ref, bias_ref, out_ref,
    a_buf, x0, x1, s_buf, o0, o1, plan_v, plan_s, agg,
    *rest,
):
    bufs, (a_sem, p_sem, gs, gr, rs, rr) = rest[:-6], rest[-6:]
    rxa, rb1l, rb1h, rbm, rbp, ra1l, ra1h, ram, rap, sxb, rxb = zip(bufs[:11], bufs[11:])
    rep, row = lax.axis_index("rep"), lax.axis_index("row")
    y, l = rep // 2, rep % 2
    h, z, c = row // 8, (row // 2) % 4, row % 2
    zp = (rep, h * 8 + ((z + 1) % 4) * 2 + c)
    zm = (rep, h * 8 + ((z + 3) % 4) * 2 + c)
    xh = (rep, (1 - h) * 8 + z * 2 + c)
    sib = (rep, h * 8 + z * 2 + (1 - c))
    xl = (y * 2 + (1 - l), row)
    yp = (((y + 1) % 4) * 2 + l, row)
    ym = (((y + 3) % 4) * 2 + l, row)
    partners = (zp, zm, xh, sib, xl, yp, ym)
    xs, outs = (x0, x1), (o0, o1)

    loads = []
    per = SLOTS // 6
    for j in range(6):
        load = pltpu.make_async_copy(
            tiles_ref.at[pl.ds(j * per, per)], a_buf.at[pl.ds(j * per, per)], a_sem.at[j]
        )
        load.start()
        loads.append(load)
    barrier = pltpu.get_barrier_semaphore()
    for device in partners:
        pl.semaphore_signal(barrier, inc=1, device_id=device, device_id_type=MESH)

    scale = lax.rsqrt(deg_ref[...].astype(F32))
    for t in range(16):
        turned = feat_ref[t * T : (t + 1) * T, :].T.astype(F32)
        scaled = (turned * scale[t : t + 1, :]).astype(BF16)
        for ch in range(CH):
            xs[ch][row * 16 + t] = scaled[FOF[ch] : FOF[ch] + FCS[ch], :]
    a_buf[SLOTS] = jnp.zeros((T, T), BF16)
    s_buf[STEPS] = jnp.zeros((max(FCS), T), BF16)

    pl.semaphore_wait(barrier, len(partners))

    def block(dh, dz, core=None):
        return ((h + dh) % 2) * 8 + ((z + dz) % 4) * 2 + (c if core is None else core)

    def g_copy(ch, k, to, blk, lo=0, hi=16):
        ref = xs[ch].at[pl.ds(blk * 16 + lo, hi - lo)]
        return pltpu.make_async_remote_copy(
            ref, ref, gs.at[ch, k], gr.at[ch, k], device_id=to, device_id_type=MESH
        )

    other = 1 - c
    G = {
        0: (zp, (0, 0), (0, 3), 0, 8),
        1: (zm, (0, 0), (0, 1), 8, 16),
        2: (xh, (0, 0), (1, 0), 0, 16),
        3: (sib, (0, 0), None, 0, 16),
        4: (zp, (0, 3), (0, 2), 0, 8),
        5: (sib, (0, 3), None, 0, 16),
        6: (zm, (0, 1), (0, 2), 8, 16),
        7: (sib, (0, 1), None, 0, 16),
        8: (zp, (1, 0), (1, 3), NX, 16),
        9: (zm, (1, 0), (1, 1), 0, 16 - NX),
        10: (sib, (1, 0), None, 0, 16),
        11: (xh, (0, 2), (1, 2), NQ, 8),
        12: (xh, (0, 2), (1, 2), 8, 16 - NQ),
        13: (sib, (0, 2), None, 0, 8),
        14: (sib, (0, 2), None, 8, 16),
        15: (sib, (1, 3), None, NX, 16),
        16: (sib, (1, 1), None, 0, 16 - NX),
        17: (sib, (1, 2), None, NQ, 8),
        18: (sib, (1, 2), None, 8, 16 - NQ),
        19: (xh, (0, 3), (1, 3), 0, NX),
        20: (xh, (0, 1), (1, 1), 16 - NX, 16),
        21: (sib, (1, 3), None, 0, NX),
        22: (sib, (1, 1), None, 16 - NX, 16),
        23: (zp, (0, 0), (0, 3), 8, 16),
        24: (zm, (0, 0), (0, 1), 0, 8),
        25: (zp, (1, 3), (1, 2), 0, NQ),
        26: (zm, (1, 1), (1, 2), 16 - NQ, 16),
        27: (sib, (1, 2), None, 0, NQ),
        28: (sib, (1, 2), None, 16 - NQ, 16),
    }
    left = {ch: set(G) for ch in range(CH)}
    r_left = {ch: set(range(23)) for ch in range(CH)}

    def g_send(ch, *ks):
        for k in ks:
            to, sent, _, lo, hi = G[k]
            g_copy(ch, k, to, block(*sent), lo, hi).start()

    def g_recv(ch, *ks):
        for k in ks:
            to, sent, got, lo, hi = G[k]
            blk = block(*sent, core=other) if got is None else block(*got)
            g_copy(ch, k, to, blk, lo, hi).wait_recv()

    def g_sent(ch, *ks):
        for k in ks:
            left[ch].remove(k)
            to, sent, _, lo, hi = G[k]
            g_copy(ch, k, to, block(*sent), lo, hi).wait_send()

    def g_first(ch):
        g_send(ch, 0, 1, 2, 3)

    def g_own(ch):
        g_sent(ch, 0, 1)
        g_send(ch, 23, 24)

    def g_second(ch):
        g_recv(ch, 0)
        g_send(ch, 4, 19)
        g_recv(ch, 1)
        g_send(ch, 6, 20)

    def g_third(ch):
        g_recv(ch, 2)
        g_sent(ch, 4, 6)
        g_send(ch, 8, 9, 10)

    def g_fourth(ch):
        g_recv(ch, 4)
        g_send(ch, 11, 13)
        g_recv(ch, 6)
        g_send(ch, 12, 14)

    def g_fifth(ch):
        g_recv(ch, 19)
        g_send(ch, 25, 21)
        g_recv(ch, 20)
        g_send(ch, 26, 22)
        g_recv(ch, 23)
        g_send(ch, 5)
        g_recv(ch, 24)
        g_send(ch, 7)

    def g_sixth(ch):
        g_recv(ch, 8)
        g_send(ch, 15)
        g_recv(ch, 9)
        g_send(ch, 16)

    def g_last(ch):
        g_recv(ch, 11)
        g_send(ch, 17)
        g_recv(ch, 12)
        g_send(ch, 18)
        g_recv(ch, 25)
        g_send(ch, 27)
        g_recv(ch, 26)
        g_send(ch, 28)
        g_recv(ch, 3, 5, 7, 10, 13, 14, 15, 16, 21, 22, 17, 18, 27, 28)

    def at_y(d):
        return (y + d) % 4

    alo, ahi = pl.ds(0, HA), pl.ds(HA, HA)
    blo, bhi = pl.ds(NA, HB), pl.ds(NA + HB, HB)
    zlo, zhi = pl.ds(0, HB), pl.ds(HB, HB)
    sides = (1 - l, l)

    def r_copy(ch, k):
        o = outs[ch]
        if k < 4:
            src, dst, to = o.at[at_y(k) * 2 + (1 - l), pl.ds(0, NA)], rxa[ch].at[k], xl
        elif k < 16:
            q = (k - 4) // 6
            where, part, dst, to = {
                0: (at_y(2), blo, rb1l[ch].at[q], ym),
                1: (at_y(2), bhi, rb1h[ch].at[q], yp),
                2: (at_y(1), blo, rbm[ch].at[q, zlo], yp),
                3: (at_y(3), bhi, rbp[ch].at[q, zhi], ym),
                4: (at_y(3), blo, rbp[ch].at[q, zlo], ym),
                5: (at_y(1), bhi, rbm[ch].at[q, zhi], yp),
            }[(k - 4) % 6]
            src = o.at[where * 2 + sides[q], part]
        elif k < 22:
            where, part, dst, to = {
                16: (at_y(2), alo, ra1l[ch], ym),
                17: (at_y(2), ahi, ra1h[ch], yp),
                18: (at_y(1), alo, ram[ch].at[alo], yp),
                19: (at_y(3), ahi, rap[ch].at[ahi], ym),
                20: (at_y(3), alo, rap[ch].at[alo], ym),
                21: (at_y(1), ahi, ram[ch].at[ahi], yp),
            }[k]
            src = o.at[where * 2 + l, part]
        else:
            src, dst, to = sxb[ch], rxb[ch], xl
        return pltpu.make_async_remote_copy(
            src, dst, rs.at[ch, k], rr.at[ch, k], device_id=to, device_id_type=MESH
        )

    def r_send(ch, *ks):
        for k in ks:
            r_copy(ch, k).start()

    def r_recv(ch, *ks):
        for k in ks:
            r_copy(ch, k).wait_recv()

    def r_sent(ch, *ks):
        for k in ks:
            r_left[ch].remove(k)
            r_copy(ch, k).wait_send()

    def add_to(ch, part, at, count, got):
        o = outs[ch]
        for t in range(count):
            o[part, at + t] = (o[part, at + t].astype(F32) + got[t].astype(F32)).astype(BF16)

    def r_first(ch):
        r_send(ch, 4, 5, 2, 6, 7)

    def r_second(ch):
        r_sent(ch, 4, 5, 2)
        r_send(ch, 10, 11, 1, 3)

    def r_third(ch):
        r_recv(ch, 4)
        add_to(ch, at_y(3) * 2 + sides[0], NA, HB, rb1l[ch].at[0])
        r_send(ch, 8)
        r_recv(ch, 5)
        add_to(ch, at_y(1) * 2 + sides[0], NA + HB, HB, rb1h[ch].at[0])
        r_send(ch, 9)
        r_recv(ch, 2)
        add_to(ch, at_y(2) * 2 + l, 0, NA, rxa[ch].at[2])
        r_send(ch, 16, 17, 0)

    def r_fourth(ch):
        r_recv(ch, 10)
        add_to(ch, at_y(3) * 2 + sides[1], NA, HB, rb1l[ch].at[1])
        r_send(ch, 14)
        r_recv(ch, 11)
        add_to(ch, at_y(1) * 2 + sides[1], NA + HB, HB, rb1h[ch].at[1])
        r_send(ch, 15, 12, 13)

    def r_fifth(ch):
        r_recv(ch, 6, 7, 8, 9)
        for t in range(NB):
            total = outs[ch][y * 2 + sides[0], NA + t].astype(F32)
            total = total + rbm[ch][0, t].astype(F32) + rbp[ch][0, t].astype(F32)
            sxb[ch][t] = total.astype(BF16)
        r_send(ch, 22)

    def r_sixth(ch):
        r_recv(ch, 1)
        add_to(ch, at_y(1) * 2 + l, 0, NA, rxa[ch].at[1])
        r_send(ch, 18)
        r_recv(ch, 3)
        add_to(ch, at_y(3) * 2 + l, 0, NA, rxa[ch].at[3])
        r_send(ch, 19)

    def r_seventh(ch):
        r_recv(ch, 16)
        add_to(ch, at_y(3) * 2 + l, 0, HA, ra1l[ch])
        r_send(ch, 20)
        r_recv(ch, 17)
        add_to(ch, at_y(1) * 2 + l, HA, HA, ra1h[ch])
        r_send(ch, 21)

    def finish(ch, t, total):
        agg[t, FOF[ch] : FOF[ch] + FCS[ch], :] = (total * lax.rsqrt(deg_ref[t : t + 1, :].astype(F32))).astype(BF16)

    def r_last(ch):
        r_recv(ch, 0, 18, 19, 20, 21)
        for t in range(NA):
            total = outs[ch][y * 2 + l, t].astype(F32) + rxa[ch][0, t].astype(F32)
            finish(ch, t, total + ram[ch][t].astype(F32) + rap[ch][t].astype(F32))
        r_recv(ch, 12, 13, 14, 15, 22)
        for t in range(NB):
            total = outs[ch][y * 2 + l, NA + t].astype(F32) + rxb[ch][t].astype(F32)
            finish(ch, NA + t, total + rbm[ch][1, t].astype(F32) + rbp[ch][1, t].astype(F32))

    def products(ch, events):
        x = xs[ch]

        def body(i, acc):
            for at, act in events:
                pl.when(i == at)(act)
            for u in range(UNROLL):
                spot = (i % 2) * (2 * UNROLL) + 2 * u
                first = jnp.clip(plan_s[i // 2, spot], 0, SLOTS * 256 + 255)
                second = jnp.clip(plan_s[i // 2, spot + 1], 0, SLOTS * 256 + 255)
                keep = plan_s[ROW_KEEP + i // 4, (i % 4) * UNROLL + u].astype(F32)
                values = jnp.concatenate([a_buf[first >> 8], a_buf[second >> 8]], axis=1)
                nodes = jnp.concatenate([x[first & 255], x[second & 255]], axis=1)
                acc = acc * keep + lax.dot_general(nodes, values, NT, preferred_element_type=F32)
                s_buf[i * UNROLL + u, 0 : FCS[ch]] = acc.astype(BF16)
            return acc

        lax.fori_loop(0, ITERS, body, jnp.zeros((FCS[ch], T), F32))

    def extract(ch):
        o = outs[ch]

        def body(i, _):
            for u in range(16):
                o[i, u] = s_buf[jnp.clip(plan_s[ROW_END, i * 16 + u], 0, STEPS), 0 : FCS[ch]]
            return 0

        lax.fori_loop(0, 8, body, 0)

    g_first(0)
    g_own(0)
    make_plan(rows_ref, cols_ref, live_ref[0], plan_v)
    to_smem = pltpu.make_async_copy(plan_v, plan_s, p_sem)
    to_smem.start()
    g_second(0)
    g_third(0)
    g_fourth(0)
    g_fifth(0)
    g_first(1)
    g_send(1, 23, 24)
    to_smem.wait()
    for load in loads:
        load.wait()
    g_sixth(0)
    g_last(0)

    products(
        0,
        [
            (4, lambda: g_second(1)),
            (7, lambda: g_third(1)),
            (9, lambda: g_fourth(1)),
            (10, lambda: g_fifth(1)),
            (12, lambda: g_sixth(1)),
        ],
    )
    extract(0)
    r_first(0)
    g_last(1)
    products(
        1,
        [
            (1, lambda: r_second(0)),
            (3, lambda: r_third(0)),
            (6, lambda: r_fourth(0)),
            (9, lambda: r_fifth(0)),
            (10, lambda: r_sixth(0)),
            (12, lambda: r_seventh(0)),
        ],
    )
    extract(1)
    r_first(1)
    r_second(1)
    r_last(0)
    r_third(1)
    r_fourth(1)
    r_fifth(1)
    r_sixth(1)
    r_seventh(1)
    r_last(1)

    def body(i, _):
        for u in range(4):
            t = i * 4 + u
            mixed = lax.dot_general(agg[t], weight_ref[...], TN, preferred_element_type=F32)
            out_ref[pl.ds(t * T, T), :] = jnp.maximum(mixed + bias_ref[...], 0.0).astype(BF16)
        return 0

    lax.fori_loop(0, 4, body, 0)
    for ch in range(CH):
        g_sent(ch, *sorted(left[ch]))
        r_sent(ch, *sorted(r_left[ch]))


def per_device(features, degrees, tile_values, tile_rows, tile_cols, tile_live, weight, bias):
    vmem = pl.BlockSpec(memory_space=pltpu.VMEM)
    landing = [(4, NA), (2, HB), (2, HB), (2, NB), (2, NB), (HA,), (HA,), (NA,), (NA,), (NB,), (NB,)]
    return pl.pallas_call(
        kernel,
        out_shape=jax.ShapeDtypeStruct(features.shape, BF16),
        in_specs=[
            vmem, vmem, pl.BlockSpec(memory_space=pl.ANY), vmem, vmem,
            pl.BlockSpec(memory_space=pltpu.SMEM), vmem, vmem,
        ],
        out_specs=vmem,
        scratch_shapes=[
            pltpu.VMEM((SLOTS + 1, T, T), BF16),
            pltpu.VMEM((256, FCS[0], T), BF16),
            pltpu.VMEM((256, FCS[1], T), BF16),
            pltpu.VMEM((STEPS + 1, max(FCS), T), BF16),
            pltpu.VMEM((8, 16, FCS[0], T), BF16),
            pltpu.VMEM((8, 16, FCS[1], T), BF16),
            pltpu.VMEM((16, T), I32),
            pltpu.SMEM((16, T), I32),
            pltpu.VMEM((16, 128, T), BF16),
            *[pltpu.VMEM(shape + (fc, T), BF16) for fc in FCS for shape in landing],
            pltpu.SemaphoreType.DMA((6,)),
            pltpu.SemaphoreType.DMA,
            pltpu.SemaphoreType.DMA((CH, 29)),
            pltpu.SemaphoreType.DMA((CH, 29)),
            pltpu.SemaphoreType.DMA((CH, 23)),
            pltpu.SemaphoreType.DMA((CH, 23)),
        ],
        compiler_params=pltpu.CompilerParams(
            collective_id=0, has_side_effects=True, vmem_limit_bytes=60 << 20
        ),
        name="graph_layer",
    )(
        features,
        degrees.reshape(16, T),
        tile_values,
        tile_rows.reshape(SLOTS // T, T),
        tile_cols.reshape(SLOTS // T, T),
        tile_live,
        weight,
        bias.reshape(1, 128),
    )


def solution(mesh):
    return jax.shard_map(
        per_device,
        mesh=mesh,
        in_specs=(
            P(("rep", "row"), None),
            P(("rep", "row")),
            P(("rep", "row"), None, None),
            P(("rep", "row")),
            P(("rep", "row")),
            P(("rep", "row")),
            P(),
            P(),
        ),
        out_specs=P(("rep", "row"), None),
        check_vma=False,
    )
```

```python
import functools

import jax
import jax.numpy as jnp
from jax import lax
from jax.experimental import pallas as pl
from jax.experimental.pallas import tpu as pltpu
from jax.sharding import PartitionSpec as P

MESH = pl.DeviceIdType.MESH
F32, BF16, I32 = jnp.float32, jnp.bfloat16, jnp.int32
NT = (((1,), (1,)), ((), ()))

T = 128
CH = 2
FC = 128 // CH
SLOTS = 768
STEPS = 448
UNROLL = 64
ITERS = STEPS // UNROLL
NX = 6
NQ = 4
NA = 7
NB = 16 - NA
HAL, HAH, HBL, HBH = 3, 4, 5, 4
ROW_KEEP, ROW_END = 8, 12


def make_plan(rows_ref, cols_ref, live, plan_ref):
    lane = lax.broadcasted_iota(I32, (T, T), 1)
    sub = lax.broadcasted_iota(I32, (T, T), 0)
    before = (sub < lane).astype(BF16)
    lane1 = lax.broadcasted_iota(I32, (1, T), 1)
    lane_f = lane.astype(F32)
    zero = jnp.zeros((T, T), F32)
    carry = jnp.zeros((T, 1), F32)
    hots, ranks, alive = [], [], []
    for j in range(SLOTS // T):
        there = (lane1 + j * T) < live
        r = jnp.where(there, rows_ref[j : j + 1, :], T)
        hot = jnp.where(sub == r, 1.0, 0.0).astype(F32)
        earlier = jnp.dot(hot.astype(BF16), before, preferred_element_type=F32)
        ranks.append(jnp.sum(hot * (earlier + carry), axis=0, keepdims=True))
        carry = carry + jnp.sum(hot, axis=1, keepdims=True)
        hots.append(hot)
        alive.append(there)
    pairs = jnp.broadcast_to(jnp.floor((carry + 1.0) * 0.5), (T, T))
    start = jnp.sum(jnp.where(lane < sub, pairs.T, zero), axis=1, keepdims=True)
    start = jnp.broadcast_to(start, (T, T))
    places, codes = [], []
    for j in range(SLOTS // T):
        place = ranks[j] + 2.0 * jnp.sum(hots[j] * start, axis=0, keepdims=True)
        places.append(jnp.where(alive[j], place, -1.0))
        codes.append(((lane1 + (j * T - SLOTS)) * 256 + cols_ref[j : j + 1, :]).astype(F32))
    fill = [jnp.full((2, T), -1.0, F32)]
    places_t = jnp.concatenate(places + fill, axis=0).T
    codes_t = jnp.concatenate(codes + fill, axis=0).T
    sums = [zero] * (2 * STEPS // T)
    for j in range(SLOTS // T):
        place = jnp.broadcast_to(places_t[:, j : j + 1], (T, T))
        code = jnp.broadcast_to(codes_t[:, j : j + 1], (T, T))
        for b in range(2 * STEPS // T):
            sums[b] = sums[b] + jnp.where(place == lane_f + float(b * T), code, zero)
    for b in range(2 * STEPS // T):
        code = jnp.sum(sums[b], axis=0, keepdims=True).astype(I32) + SLOTS * 256
        plan_ref[b : b + 1, :] = jnp.clip(code, 0, SLOTS * 256 + 255)
    for b in range(4):
        begins = jnp.where((start == lane_f + float(b * T)) & (pairs > 0.0), 1.0, 0.0)
        plan_ref[ROW_KEEP + b : ROW_KEEP + b + 1, :] = 1 - jnp.sum(begins, axis=0, keepdims=True).astype(I32)
    ends = jnp.where(pairs > 0.0, start + pairs - 1.0, float(STEPS))
    plan_ref[ROW_END : ROW_END + 1, :] = jnp.clip(ends.T[0:1, :].astype(I32), 0, STEPS)


def kernel(
    feat_ref, deg_ref, tiles_ref, rows_ref, cols_ref, live_ref, agg,
    a_buf, x0, x1, s_buf, o0, o1, plan_v, plan_s, scales,
    *rest,
):
    bufs, (a_sem, p_sem, gs, gr, rs, rr) = rest[:-6], rest[-6:]
    rxa, rb1l, rb1h, rbm, rbp, ra1l, ra1h, ram, rap, sxb, rxb = zip(bufs[:11], bufs[11:])
    rep, row = lax.axis_index("rep"), lax.axis_index("row")
    y, l = rep // 2, rep % 2
    h, z, c = row // 8, (row // 2) % 4, row % 2
    zp = (rep, h * 8 + ((z + 1) % 4) * 2 + c)
    zm = (rep, h * 8 + ((z + 3) % 4) * 2 + c)
    xh = (rep, (1 - h) * 8 + z * 2 + c)
    sib = (rep, h * 8 + z * 2 + (1 - c))
    xl = (y * 2 + (1 - l), row)
    yp = (((y + 1) % 4) * 2 + l, row)
    ym = (((y + 3) % 4) * 2 + l, row)
    partners = (zp, zm, xh, sib, xl, yp, ym)
    xs, outs = (x0, x1), (o0, o1)

    loads = []
    per = SLOTS // 6
    for j in range(6):
        load = pltpu.make_async_copy(
            tiles_ref.at[pl.ds(j * per, per)], a_buf.at[pl.ds(j * per, per)], a_sem.at[j]
        )
        load.start()
        loads.append(load)
    barrier = pltpu.get_barrier_semaphore()
    for device in partners:
        pl.semaphore_signal(barrier, inc=1, device_id=device, device_id_type=MESH)

    scale = lax.rsqrt(deg_ref[...].astype(F32))
    for t in range(16):
        turned = feat_ref[t * T : (t + 1) * T, :].T.astype(F32)
        scaled = (turned * scale[t : t + 1, :]).astype(BF16)
        for ch in range(CH):
            xs[ch][row * 16 + t] = scaled[ch * FC : (ch + 1) * FC, :]
    columns = jnp.concatenate([scale] * 8, axis=0).T
    for t in range(0, 16, 2):
        pair = [jnp.broadcast_to(columns[:, t + side : t + side + 1], (T, FC)) for side in range(2)]
        pair = jnp.concatenate(pair, axis=1)
        scales[t], scales[t + 1] = pair[: T // 2], pair[T // 2 :]
    a_buf[SLOTS] = jnp.zeros((T, T), BF16)
    s_buf[STEPS] = jnp.zeros((T, FC), BF16)

    pl.semaphore_wait(barrier, len(partners))

    def block(dh, dz, core=None):
        return ((h + dh) % 2) * 8 + ((z + dz) % 4) * 2 + (c if core is None else core)

    def g_copy(ch, k, to, blk, lo=0, hi=16):
        ref = xs[ch].at[pl.ds(blk * 16 + lo, hi - lo)]
        return pltpu.make_async_remote_copy(
            ref, ref, gs.at[ch, k], gr.at[ch, k], device_id=to, device_id_type=MESH
        )

    other = 1 - c
    G = {
        0: (zp, (0, 0), (0, 3), 0, 8),
        1: (zm, (0, 0), (0, 1), 8, 16),
        2: (xh, (0, 0), (1, 0), 0, 16),
        3: (sib, (0, 0), None, 0, 16),
        4: (zp, (0, 3), (0, 2), 0, 8),
        5: (sib, (0, 3), None, 0, 16),
        6: (zm, (0, 1), (0, 2), 8, 16),
        7: (sib, (0, 1), None, 0, 16),
        8: (zp, (1, 0), (1, 3), NX, 16),
        9: (zm, (1, 0), (1, 1), 0, 16 - NX),
        10: (sib, (1, 0), None, 0, 16),
        11: (xh, (0, 2), (1, 2), NQ, 8),
        12: (xh, (0, 2), (1, 2), 8, 16 - NQ),
        13: (sib, (0, 2), None, 0, 8),
        14: (sib, (0, 2), None, 8, 16),
        15: (sib, (1, 3), None, NX, 16),
        16: (sib, (1, 1), None, 0, 16 - NX),
        17: (sib, (1, 2), None, NQ, 8),
        18: (sib, (1, 2), None, 8, 16 - NQ),
        19: (xh, (0, 3), (1, 3), 0, NX),
        20: (xh, (0, 1), (1, 1), 16 - NX, 16),
        21: (sib, (1, 3), None, 0, NX),
        22: (sib, (1, 1), None, 16 - NX, 16),
        23: (zp, (0, 0), (0, 3), 8, 16),
        24: (zm, (0, 0), (0, 1), 0, 8),
        25: (zp, (1, 3), (1, 2), 0, NQ),
        26: (zm, (1, 1), (1, 2), 16 - NQ, 16),
        27: (sib, (1, 2), None, 0, NQ),
        28: (sib, (1, 2), None, 16 - NQ, 16),
    }
    left = {ch: set(G) for ch in range(CH)}
    r_left = {ch: set(range(23)) for ch in range(CH)}

    def g_send(ch, *ks):
        for k in ks:
            to, sent, _, lo, hi = G[k]
            g_copy(ch, k, to, block(*sent), lo, hi).start()

    def g_recv(ch, *ks):
        for k in ks:
            to, sent, got, lo, hi = G[k]
            blk = block(*sent, core=other) if got is None else block(*got)
            g_copy(ch, k, to, blk, lo, hi).wait_recv()

    def g_sent(ch, *ks):
        for k in ks:
            left[ch].remove(k)
            to, sent, _, lo, hi = G[k]
            g_copy(ch, k, to, block(*sent), lo, hi).wait_send()

    def g_first(ch):
        g_send(ch, 0, 1, 2, 3)

    def g_own(ch):
        g_sent(ch, 0, 1)
        g_send(ch, 23, 24)

    def g_second(ch):
        g_recv(ch, 0)
        g_send(ch, 4, 19)
        g_recv(ch, 1)
        g_send(ch, 6, 20)

    def g_third(ch):
        g_recv(ch, 2)
        g_sent(ch, 4, 6)
        g_send(ch, 8, 9, 10)

    def g_fourth(ch):
        g_recv(ch, 4)
        g_send(ch, 11, 13)
        g_recv(ch, 6)
        g_send(ch, 12, 14)

    def g_fifth(ch):
        g_recv(ch, 19)
        g_send(ch, 25, 21)
        g_recv(ch, 20)
        g_send(ch, 26, 22)
        g_recv(ch, 23)
        g_send(ch, 5)
        g_recv(ch, 24)
        g_send(ch, 7)

    def g_sixth(ch):
        g_recv(ch, 8)
        g_send(ch, 15)
        g_recv(ch, 9)
        g_send(ch, 16)

    def g_last(ch):
        g_recv(ch, 11)
        g_send(ch, 17)
        g_recv(ch, 12)
        g_send(ch, 18)
        g_recv(ch, 25)
        g_send(ch, 27)
        g_recv(ch, 26)
        g_send(ch, 28)
        g_recv(ch, 3, 5, 7, 10, 13, 14, 15, 16, 21, 22, 17, 18, 27, 28)

    def at_y(d):
        return (y + d) % 4

    alo, ahi = pl.ds(0, HAL), pl.ds(HAL, HAH)
    blo, bhi = pl.ds(NA, HBL), pl.ds(NA + HBL, HBH)
    zlo, zhi = pl.ds(0, HBL), pl.ds(HBL, HBH)
    sides = (1 - l, l)

    def r_copy(ch, k):
        o = outs[ch]
        if k < 4:
            src, dst, to = o.at[at_y(k) * 2 + (1 - l), pl.ds(0, NA)], rxa[ch].at[k], xl
        elif k < 16:
            q = (k - 4) // 6
            where, part, dst, to = {
                0: (at_y(2), blo, rb1l[ch].at[q], ym),
                1: (at_y(2), bhi, rb1h[ch].at[q], yp),
                2: (at_y(1), blo, rbm[ch].at[q, zlo], yp),
                3: (at_y(3), bhi, rbp[ch].at[q, zhi], ym),
                4: (at_y(3), blo, rbp[ch].at[q, zlo], ym),
                5: (at_y(1), bhi, rbm[ch].at[q, zhi], yp),
            }[(k - 4) % 6]
            src = o.at[where * 2 + sides[q], part]
        elif k < 22:
            where, part, dst, to = {
                16: (at_y(2), alo, ra1l[ch], ym),
                17: (at_y(2), ahi, ra1h[ch], yp),
                18: (at_y(1), alo, ram[ch].at[alo], yp),
                19: (at_y(3), ahi, rap[ch].at[ahi], ym),
                20: (at_y(3), alo, rap[ch].at[alo], ym),
                21: (at_y(1), ahi, ram[ch].at[ahi], yp),
            }[k]
            src = o.at[where * 2 + l, part]
        else:
            src, dst, to = sxb[ch], rxb[ch], xl
        return pltpu.make_async_remote_copy(
            src, dst, rs.at[ch, k], rr.at[ch, k], device_id=to, device_id_type=MESH
        )

    def r_send(ch, *ks):
        for k in ks:
            r_copy(ch, k).start()

    def r_recv(ch, *ks):
        for k in ks:
            r_copy(ch, k).wait_recv()

    def r_sent(ch, *ks):
        for k in ks:
            r_left[ch].remove(k)
            r_copy(ch, k).wait_send()

    def add_to(ch, part, at, count, got):
        o = outs[ch]
        for t in range(count):
            o[part, at + t] = (o[part, at + t].astype(F32) + got[t].astype(F32)).astype(BF16)

    def r_first(ch):
        r_send(ch, 4, 5, 2, 6, 7)

    def r_second(ch):
        r_sent(ch, 4, 5, 2)
        r_send(ch, 10, 11, 1, 3)

    def r_third(ch):
        r_recv(ch, 4)
        add_to(ch, at_y(3) * 2 + sides[0], NA, HBL, rb1l[ch].at[0])
        r_send(ch, 8)
        r_recv(ch, 5)
        add_to(ch, at_y(1) * 2 + sides[0], NA + HBL, HBH, rb1h[ch].at[0])
        r_send(ch, 9)
        r_recv(ch, 2)
        add_to(ch, at_y(2) * 2 + l, 0, NA, rxa[ch].at[2])
        r_send(ch, 16, 17, 0)

    def r_fourth(ch):
        r_recv(ch, 10)
        add_to(ch, at_y(3) * 2 + sides[1], NA, HBL, rb1l[ch].at[1])
        r_send(ch, 14)
        r_recv(ch, 11)
        add_to(ch, at_y(1) * 2 + sides[1], NA + HBL, HBH, rb1h[ch].at[1])
        r_send(ch, 15, 12, 13)

    def r_fifth(ch):
        r_recv(ch, 6, 7, 8, 9)
        for t in range(NB):
            total = outs[ch][y * 2 + sides[0], NA + t].astype(F32)
            total = total + rbm[ch][0, t].astype(F32) + rbp[ch][0, t].astype(F32)
            sxb[ch][t] = total.astype(BF16)
        r_send(ch, 22)

    def r_sixth(ch):
        r_recv(ch, 1)
        add_to(ch, at_y(1) * 2 + l, 0, NA, rxa[ch].at[1])
        r_send(ch, 18)
        r_recv(ch, 3)
        add_to(ch, at_y(3) * 2 + l, 0, NA, rxa[ch].at[3])
        r_send(ch, 19)

    def r_seventh(ch):
        r_recv(ch, 16)
        add_to(ch, at_y(3) * 2 + l, 0, HAL, ra1l[ch])
        r_send(ch, 20)
        r_recv(ch, 17)
        add_to(ch, at_y(1) * 2 + l, HAL, HAH, ra1h[ch])
        r_send(ch, 21)

    def finish(ch, t, total):
        rows, at = pl.ds((t % 2) * (T // 2), T // 2), t - t % 2
        done = (total * scales[t]).astype(BF16)
        agg[at, rows, ch * FC : (ch + 1) * FC] = done[:, :FC]
        agg[at + 1, rows, ch * FC : (ch + 1) * FC] = done[:, FC:]

    def r_last(ch):
        r_recv(ch, 0, 18, 19, 20, 21)
        for t in range(NA):
            total = outs[ch][y * 2 + l, t].astype(F32) + rxa[ch][0, t].astype(F32)
            finish(ch, t, total + ram[ch][t].astype(F32) + rap[ch][t].astype(F32))
        r_recv(ch, 12, 13, 14, 15, 22)
        for t in range(NB):
            total = outs[ch][y * 2 + l, NA + t].astype(F32) + rxb[ch][t].astype(F32)
            finish(ch, NA + t, total + rbm[ch][1, t].astype(F32) + rbp[ch][1, t].astype(F32))

    def products(ch, events):
        x = xs[ch]

        def body(i, acc):
            for at, act in events:
                pl.when(i == at)(act)
            for u in range(UNROLL):
                a_row = 64 // UNROLL
                spot = (i % a_row) * (2 * UNROLL) + 2 * u
                first = jnp.clip(plan_s[i // a_row, spot], 0, SLOTS * 256 + 255)
                second = jnp.clip(plan_s[i // a_row, spot + 1], 0, SLOTS * 256 + 255)
                keep = plan_s[ROW_KEEP + i // (2 * a_row), (i % (2 * a_row)) * UNROLL + u].astype(F32)
                values = jnp.concatenate([a_buf[first >> 8], a_buf[second >> 8]], axis=1)
                nodes = jnp.concatenate([x[first & 255], x[second & 255]], axis=1)
                acc = acc * keep + lax.dot_general(values, nodes, NT, preferred_element_type=F32)
                s_buf[i * UNROLL + u] = acc.astype(BF16)
            return acc

        lax.fori_loop(0, ITERS, body, jnp.zeros((T, FC), F32))

    def extract(ch):
        o = outs[ch]

        def body(i, _):
            for u in range(0, 16, 2):
                ends = [jnp.clip(plan_s[ROW_END, i * 16 + u + side], 0, STEPS) for side in range(2)]
                pair = jnp.concatenate([s_buf[ends[0]], s_buf[ends[1]]], axis=1)
                o[i, u], o[i, u + 1] = pair[: T // 2], pair[T // 2 :]
            return 0

        lax.fori_loop(0, 8, body, 0)

    g_first(0)
    g_own(0)
    make_plan(rows_ref, cols_ref, live_ref[0], plan_v)
    to_smem = pltpu.make_async_copy(plan_v, plan_s, p_sem)
    to_smem.start()
    g_second(0)
    g_third(0)
    g_fourth(0)
    g_fifth(0)
    g_first(1)
    g_send(1, 23, 24)
    to_smem.wait()
    for load in loads:
        load.wait()
    g_sixth(0)
    g_last(0)

    products(
        0,
        [
            (2, lambda: g_second(1)),
            (4, lambda: g_third(1)),
            (5, lambda: g_fourth(1)),
            (5, lambda: g_fifth(1)),
            (6, lambda: g_sixth(1)),
        ],
    )
    extract(0)
    r_first(0)
    g_last(1)
    products(
        1,
        [
            (0, lambda: r_second(0)),
            (2, lambda: r_third(0)),
            (3, lambda: r_fourth(0)),
            (5, lambda: r_fifth(0)),
            (5, lambda: r_sixth(0)),
            (6, lambda: r_seventh(0)),
        ],
    )
    extract(1)
    r_first(1)
    r_second(1)
    r_last(0)
    r_third(1)
    r_fourth(1)
    r_fifth(1)
    r_sixth(1)
    r_seventh(1)
    r_last(1)

    for ch in range(CH):
        g_sent(ch, *sorted(left[ch]))
        r_sent(ch, *sorted(r_left[ch]))


def per_device(features, degrees, tile_values, tile_rows, tile_cols, tile_live, weight, bias):
    vmem = pl.BlockSpec(memory_space=pltpu.VMEM)
    half = (T // 2, T)
    landing = [(4, NA), (2, HBL), (2, HBH), (2, NB), (2, NB), (HAL,), (HAH,), (NA,), (NA,), (NB,), (NB,)]
    aggregated = pl.pallas_call(
        kernel,
        out_shape=jax.ShapeDtypeStruct((16, T, 128), BF16),
        in_specs=[
            vmem, vmem, pl.BlockSpec(memory_space=pl.ANY), vmem, vmem,
            pl.BlockSpec(memory_space=pltpu.SMEM),
        ],
        out_specs=vmem,
        scratch_shapes=[
            pltpu.VMEM((SLOTS + 1, T, T), BF16),
            pltpu.VMEM((256, FC, T), BF16),
            pltpu.VMEM((256, FC, T), BF16),
            pltpu.VMEM((STEPS + 1, T, FC), BF16),
            pltpu.VMEM((8, 16) + half, BF16),
            pltpu.VMEM((8, 16) + half, BF16),
            pltpu.VMEM((16, T), I32),
            pltpu.SMEM((16, T), I32),
            pltpu.VMEM((16,) + half, F32),
            *[pltpu.VMEM(shape + half, BF16) for _ in range(CH) for shape in landing],
            pltpu.SemaphoreType.DMA((6,)),
            pltpu.SemaphoreType.DMA,
            pltpu.SemaphoreType.DMA((CH, 29)),
            pltpu.SemaphoreType.DMA((CH, 29)),
            pltpu.SemaphoreType.DMA((CH, 23)),
            pltpu.SemaphoreType.DMA((CH, 23)),
        ],
        compiler_params=pltpu.CompilerParams(
            collective_id=0, has_side_effects=True, vmem_limit_bytes=60 << 20
        ),
        name="graph_layer",
    )(
        features,
        degrees.reshape(16, T),
        tile_values,
        tile_rows.reshape(SLOTS // T, T),
        tile_cols.reshape(SLOTS // T, T),
        tile_live,
    )
    mixed = jnp.dot(aggregated.reshape(features.shape), weight, preferred_element_type=F32)
    return jnp.maximum(mixed + bias[None, :], 0.0).astype(BF16)


def solution(mesh):
    return jax.shard_map(
        per_device,
        mesh=mesh,
        in_specs=(
            P(("rep", "row"), None),
            P(("rep", "row")),
            P(("rep", "row"), None, None),
            P(("rep", "row")),
            P(("rep", "row")),
            P(("rep", "row")),
            P(),
            P(),
        ),
        out_specs=P(("rep", "row"), None),
        check_vma=False,
    )
```
